512 devices in a mesh: row: 16 (over z), col: 8 (over y, x_hi), rep: 4 (over x_lo, core).
Axes of the slice: x: 4 (x_hi: 2, x_lo: 2; x = x_hi * 2 + x_lo), y: 4, z: 16, core: 2. Of those that a mesh axis runs over, the one named last changes fastest.
Arguments:
- image_acts: bfloat16 [32768, 1152], P(('row', 'col', 'rep')), may hold values from -320 to 320, as said below
- text_acts: bfloat16 [32768, 1152], P(('row', 'col', 'rep')), may hold values from -320 to 320, as said below
- image_gain: float32 [1152], replicated, may hold values from 0.1 to 1.9
- image_offset: float32 [1152], replicated, may hold values from -3 to 3
- text_gain: float32 [1152], replicated, may hold values from 0.1 to 1.9
- text_offset: float32 [1152], replicated, may hold values from -3 to 3
Outputs:
- image_grad: bfloat16 [32768, 1152], P(('row', 'col', 'rep'))
- text_grad: bfloat16 [32768, 1152], P(('row', 'col', 'rep'))
The draws below stay inside these ranges and needn't reach their ends.
Inputs may be any that keep to these rules, and one draw needn't show every extreme that they name: `image_acts`: cached activations of the image tower. `text_acts`: cached activations of the text tower.
All inputs are finite; a program needn't handle non-finite values.
Results may differ from the reference program's by a relative error of at most 0.0081.
Values may be sent and summed in bfloat16 or wider, within the bound.
No kernel may reach another device: no remote copies, remote signals or barrier semaphores. Data moves between devices by JAX's collectives and lax.ppermute only.
A program may use at most 64 MiB of HBM per device.

```python
import math
import jax
import jax.numpy as jnp
from jax import lax

D = 1152
GROUP = 64
PAIRS = 32768
N_ROW = 16
N_COL = 8
N_REP = 4


class_count = 64


def shared_rows(key):
    class_ids = jax.random.randint(jax.random.fold_in(key, 500), (PAIRS,), 0, class_count)
    prototypes = jax.random.truncated_normal(jax.random.fold_in(key, 501), -4.0, 4.0, (class_count, D), jnp.float32)
    return jnp.take(prototypes, class_ids, axis=0)


def assemble(key, shared, noise_part, mixing, top_scale):
    row_scale = jnp.exp(jax.random.uniform(jax.random.fold_in(key, 3), (PAIRS, 1), jnp.float32, 0.0, math.log(top_scale)))
    column_scale = jnp.exp(jax.random.uniform(jax.random.fold_in(key, 4), (1, D), jnp.float32, math.log(0.5), math.log(2.0)))
    return (row_scale * column_scale * (mixing * shared + noise_part)).astype(jnp.bfloat16)


def draw_image_acts(key, part):
    shared = shared_rows(key)
    key = jax.random.fold_in(key, 1)
    noise_part = jax.random.truncated_normal(jax.random.fold_in(key, 2), -4.0, 4.0, (PAIRS, D), jnp.float32)
    return assemble(key, shared, noise_part, 1.5, 10.0)


def draw_text_acts(key, part):
    shared = shared_rows(key)
    key = jax.random.fold_in(key, 11)
    noise_part = jax.random.truncated_normal(jax.random.fold_in(key, 2), -4.0, 4.0, (PAIRS, D), jnp.float32)
    return assemble(key, shared, noise_part, 1.5, 10.0)


def scatter_about(own_key, dims, spread, most, held_as=jnp.bfloat16):
    drawn = jax.random.normal(own_key, dims, jnp.float32) * spread
    return jnp.minimum(jnp.maximum(drawn, -most), most).astype(held_as)


def setup_inputs(seed: int = 0) -> dict:
    arg_keys = jax.random.split(jax.random.key(seed), 7)
    image_acts = draw_image_acts(jax.random.fold_in(arg_keys[6], 71), 0)
    text_acts = draw_text_acts(jax.random.fold_in(arg_keys[6], 71), 0)
    image_gain = jnp.clip(1.0 + 0.18 * jax.random.normal(arg_keys[2], (D,), jnp.float32), 0.1, 1.9)
    image_offset = scatter_about(arg_keys[3], (D,), 0.5, 3.0, jnp.float32)
    text_gain = jnp.clip(1.0 + 0.18 * jax.random.normal(arg_keys[4], (D,), jnp.float32), 0.1, 1.9)
    text_offset = scatter_about(arg_keys[5], (D,), 0.5, 3.0, jnp.float32)
    return dict(image_acts=image_acts, text_acts=text_acts, image_gain=image_gain, image_offset=image_offset, text_gain=text_gain, text_offset=text_offset)


logit_scale = 10.0
logit_shift = -10.0
loss_weight = 16.0
norm_eps = 1e-06
unit_eps = 1e-06

def normalize(acts, gains, offset):
    values = acts.astype(jnp.float32)
    row_mean = lax.optimization_barrier(jnp.mean(values, axis=-1, keepdims=True))
    centered = values - row_mean
    row_var = lax.optimization_barrier(jnp.mean(centered * centered, axis=-1, keepdims=True))
    inverse_std = lax.rsqrt(row_var + norm_eps)
    hat_rows = centered * inverse_std
    scaled = hat_rows * gains + offset
    inverse_len = lax.rsqrt(lax.optimization_barrier(jnp.sum(scaled * scaled, axis=-1, keepdims=True)) + unit_eps)
    return (scaled * inverse_len, hat_rows, inverse_std, inverse_len)

def norm_backward(unit_grad, unit_rows, hat_rows, inverse_std, inverse_len, gains):
    along = lax.optimization_barrier(jnp.sum(unit_rows * unit_grad, axis=-1, keepdims=True))
    grad_scaled = (unit_grad - unit_rows * along) * inverse_len
    grad_hat = grad_scaled * gains
    mean_one = lax.optimization_barrier(jnp.mean(grad_hat, axis=-1, keepdims=True))
    mean_two = lax.optimization_barrier(jnp.mean(grad_hat * hat_rows, axis=-1, keepdims=True))
    return inverse_std * (grad_hat - mean_one - hat_rows * mean_two)

def replica_grads(image_rows, text_rows):
    total_rows = image_rows.shape[0]
    block_rows = math.gcd(total_rows, 1024)
    block_count = total_rows // block_rows

    def block_pass(text_sum, block_index):
        first_row = (block_index * block_rows).astype(jnp.int32)
        image_block = lax.dynamic_slice_in_dim(image_rows, first_row, block_rows, 0)
        scores = jnp.dot(image_block, text_rows.T, preferred_element_type=jnp.float32)
        fixed_index = lax.broadcasted_iota(jnp.int32, scores.shape, 0) + first_row
        moving_index = lax.broadcasted_iota(jnp.int32, scores.shape, 1)
        labels = jnp.where(fixed_index == moving_index, jnp.float32(1.0), jnp.float32(0.0))
        pair_grad = (loss_weight * (jax.nn.sigmoid(logit_scale * scores + logit_shift) - labels)).astype(jnp.bfloat16)
        image_part = logit_scale * jnp.dot(pair_grad, text_rows, preferred_element_type=jnp.float32)
        text_sum = text_sum + logit_scale * jnp.dot(pair_grad.T, image_block, preferred_element_type=jnp.float32)
        return (text_sum, image_part)
    start_sum = jnp.zeros(text_rows.shape, jnp.float32)
    text_sum, image_parts = lax.scan(block_pass, start_sum, jnp.arange(block_count, dtype=jnp.int32))
    return (image_parts.reshape(total_rows, text_rows.shape[1]), text_sum)

def reference(image_acts, text_acts, image_gain, image_offset, text_gain, text_offset):
    image_unit, image_hat, image_std, image_len = normalize(image_acts, image_gain, image_offset)
    text_unit, text_hat, text_std, text_len = normalize(text_acts, text_gain, text_offset)
    image_embed = image_unit.astype(jnp.bfloat16)
    text_embed = text_unit.astype(jnp.bfloat16)
    width = image_acts.shape[1]
    total_rows = N_ROW * N_COL * GROUP
    image_shaped = image_embed.reshape(N_ROW, N_COL, N_REP, GROUP, width)
    text_shaped = text_embed.reshape(N_ROW, N_COL, N_REP, GROUP, width)
    image_list = []
    text_list = []
    for replica in range(N_REP):
        image_rows = image_shaped[:, :, replica].reshape(total_rows, width)
        text_rows = text_shaped[:, :, replica].reshape(total_rows, width)
        image_part, text_part = replica_grads(image_rows, text_rows)
        image_list.append(image_part.reshape(N_ROW, N_COL, GROUP, width))
        text_list.append(text_part.reshape(N_ROW, N_COL, GROUP, width))
    image_unit_grad = jnp.stack(image_list, axis=2).reshape(image_acts.shape)
    text_unit_grad = jnp.stack(text_list, axis=2).reshape(text_acts.shape)
    image_grad = norm_backward(image_unit_grad, image_unit, image_hat, image_std, image_len, image_gain)
    text_grad = norm_backward(text_unit_grad, text_unit, text_hat, text_std, text_len, text_gain)
    return (image_grad.astype(jnp.bfloat16), text_grad.astype(jnp.bfloat16))
```

```python
import jax
import jax.numpy as jnp
from jax import lax
from jax.experimental import pallas as pl
from jax.experimental.pallas import tpu as pltpu
from jax.sharding import PartitionSpec as P

logit_scale = 10.0
logit_shift = -10.0
loss_weight = 16.0
norm_eps = 1e-06
unit_eps = 1e-06
row_blocks = 4


def normalize(acts, gains, offset):
    values = acts.astype(jnp.float32)
    row_mean = jnp.mean(values, axis=-1, keepdims=True)
    centered = values - row_mean
    row_var = jnp.mean(centered * centered, axis=-1, keepdims=True)
    inverse_std = lax.rsqrt(row_var + norm_eps)
    hat_rows = centered * inverse_std
    scaled = hat_rows * gains + offset
    inverse_len = lax.rsqrt(jnp.sum(scaled * scaled, axis=-1, keepdims=True) + unit_eps)
    return (scaled * inverse_len, hat_rows, inverse_std, inverse_len)


def norm_backward(unit_grad, unit_rows, hat_rows, inverse_std, inverse_len, gains):
    along = jnp.sum(unit_rows * unit_grad, axis=-1, keepdims=True)
    grad_scaled = (unit_grad - unit_rows * along) * inverse_len
    grad_hat = grad_scaled * gains
    mean_one = jnp.mean(grad_hat, axis=-1, keepdims=True)
    mean_two = jnp.mean(grad_hat * hat_rows, axis=-1, keepdims=True)
    return inverse_std * (grad_hat - mean_one - hat_rows * mean_two)


def embed_kernel(image_ref, text_ref, ig_ref, io_ref, tg_ref, to_ref, out_ref):
    image_unit = normalize(image_ref[...], ig_ref[...], io_ref[...])[0]
    text_unit = normalize(text_ref[...], tg_ref[...], to_ref[...])[0]
    out_ref[0] = image_unit.astype(jnp.bfloat16)
    out_ref[1] = text_unit.astype(jnp.bfloat16)


def embed(image_acts, text_acts, ig, io, tg, to):
    rows, width = image_acts.shape
    return pl.pallas_call(
        embed_kernel,
        out_shape=jax.ShapeDtypeStruct((2, rows, width), jnp.bfloat16),
    )(image_acts, text_acts, ig, io, tg, to)


def pair_kernel(place_ref, fixed_ref, moving_ref, out_ref, total):
    step = pl.program_id(1)
    planes, _, group, width = moving_ref.shape
    blocks = fixed_ref.shape[0]
    fixed = fixed_ref[...].reshape(blocks * group, width)
    moving = moving_ref[...].reshape(planes * group, width)
    scores = lax.dot_general(
        fixed, moving, (((1,), (1,)), ((), ())), preferred_element_type=jnp.float32
    )
    fixed_index = lax.broadcasted_iota(jnp.int32, scores.shape, 0) - place_ref[1] * group
    moving_index = lax.broadcasted_iota(jnp.int32, scores.shape, 1)
    moving_index = moving_index + (step * planes - place_ref[0]) * group
    own = jnp.logical_and(
        fixed_index == moving_index,
        jnp.logical_and(fixed_index >= 0, fixed_index < group),
    )
    labels = jnp.where(own, jnp.float32(1.0), jnp.float32(0.0))
    pair_grad = (jax.nn.sigmoid(logit_scale * scores + logit_shift) - labels).astype(jnp.bfloat16)
    part = jnp.dot(pair_grad, moving, preferred_element_type=jnp.float32)

    @pl.when(step == 0)
    def _():
        total[...] = part

    @pl.when(step > 0)
    def _():
        total[...] += part

    @pl.when(step == pl.num_programs(1) - 1)
    def _():
        out_ref[...] = total[...].astype(jnp.bfloat16).reshape(out_ref.shape)


def pair_grads(place, fixed, moving):
    blocks, towers, group, width = fixed.shape
    planes = moving.shape[0]
    steps = row_blocks
    per_step = planes // steps
    flops = 4 * towers * blocks * planes * group * group * width
    return pl.pallas_call(
        pair_kernel,
        out_shape=jax.ShapeDtypeStruct((blocks, towers, group, width), jnp.bfloat16),
        grid_spec=pltpu.PrefetchScalarGridSpec(
            num_scalar_prefetch=1,
            grid=(towers, steps),
            in_specs=[
                pl.BlockSpec((blocks, 1, group, width), lambda t, s, place: (0, t, 0, 0)),
                pl.BlockSpec((per_step, 1, group, width), lambda t, s, place: (s, 1 - t, 0, 0)),
            ],
            out_specs=pl.BlockSpec((blocks, 1, group, width), lambda t, s, place: (0, t, 0, 0)),
            scratch_shapes=[pltpu.VMEM((blocks * group, width), jnp.float32)],
        ),
        compiler_params=pltpu.CompilerParams(vmem_limit_bytes=40 * 1024 * 1024),
        cost_estimate=pl.CostEstimate(
            flops=flops, bytes_accessed=12 * 1024 * 1024, transcendentals=1024 * 1024
        ),
    )(place, fixed, moving)


def finish_kernel(
    parts_ref, image_ref, text_ref, ig_ref, io_ref, tg_ref, to_ref, image_out, text_out
):
    parts = parts_ref[...].astype(jnp.float32)
    grads = jnp.sum(parts, axis=0) * (logit_scale * loss_weight)
    sides = (
        (grads[0], image_ref, ig_ref, io_ref, image_out),
        (grads[1], text_ref, tg_ref, to_ref, text_out),
    )
    for grad, acts_ref, gain_ref, offset_ref, out_ref in sides:
        gains = gain_ref[...]
        unit, hat, std, length = normalize(acts_ref[...], gains, offset_ref[...])
        out_ref[...] = norm_backward(grad, unit, hat, std, length, gains).astype(jnp.bfloat16)


def finish(parts, image_acts, text_acts, ig, io, tg, to):
    blocks, towers, group, width = parts.shape
    rows = 16
    acts_spec = pl.BlockSpec((rows, width), lambda i: (i, 0))
    flat_spec = pl.BlockSpec((1, width), lambda i: (0, 0))
    shape = jax.ShapeDtypeStruct((group, width), jnp.bfloat16)
    return pl.pallas_call(
        finish_kernel,
        out_shape=(shape, shape),
        grid=(group // rows,),
        in_specs=[
            pl.BlockSpec((blocks, towers, rows, width), lambda i: (0, 0, i, 0)),
            acts_spec,
            acts_spec,
            flat_spec,
            flat_spec,
            flat_spec,
            flat_spec,
        ],
        out_specs=(acts_spec, acts_spec),
    )(parts, image_acts, text_acts, ig, io, tg, to)


def body(image_acts, text_acts, image_gain, image_offset, text_gain, text_offset):
    vectors = [v[None, :] for v in (image_gain, image_offset, text_gain, text_offset)]
    own = embed(image_acts, text_acts, *vectors)
    columns = lax.axis_size("col")
    moving = lax.all_gather(own, "row", axis=0)
    copies = jnp.broadcast_to(own[None], (columns, *own.shape))
    fixed = lax.all_to_all(copies, "col", 0, 0)
    place = jnp.stack([lax.axis_index("row"), lax.axis_index("col")]).astype(jnp.int32)
    parts = pair_grads(place, fixed, moving)
    parts = lax.all_to_all(parts, "col", 0, 0)
    return finish(parts, image_acts, text_acts, *vectors)


def solution(mesh):
    placed = (P(("row", "col", "rep"), None), P(("row", "col", "rep"), None), P(), P(), P(), P())
    return jax.shard_map(
        body,
        mesh=mesh,
        in_specs=placed,
        out_specs=(P(("row", "col", "rep"), None), P(("row", "col", "rep"), None)),
        check_vma=False,
    )
```

```python
import functools

import jax
import jax.numpy as jnp
from jax import lax
from jax.experimental import pallas as pl
from jax.experimental.pallas import tpu as pltpu
from jax.sharding import PartitionSpec as P

logit_scale = 10.0
logit_shift = -10.0
loss_weight = 16.0
norm_eps = 1e-06
unit_eps = 1e-06
log2_e = 1.4426950408889634
carry_scale = 32768.0
lanes = 128
chunk_rows = 16
block_rows = 256
ring_order = (0, 2, 4, 6, 7, 5, 3, 1)
last_last = (((1,), (1,)), ((), ()))


def split_three(value):
    first = value.astype(jnp.bfloat16)
    rest = value - first.astype(jnp.float32)
    second = rest.astype(jnp.bfloat16)
    third = (rest - second.astype(jnp.float32)).astype(jnp.bfloat16)
    return [part.astype(jnp.float32) for part in (first, second, third)]


def prepare_kernel(image_ref, text_ref, ig_ref, io_ref, tg_ref, to_ref, unit_ref, rows_ref):
    width = image_ref.shape[1]
    sides = ((image_ref, ig_ref, io_ref), (text_ref, tg_ref, to_ref))
    for tower, (acts_ref, gain_ref, offset_ref) in enumerate(sides):
        acts = acts_ref[...]
        gains = gain_ref[...].reshape(1, width)
        offset = offset_ref[...].reshape(1, width)
        values = acts.astype(jnp.float32)
        row_mean = jnp.mean(values, axis=-1, keepdims=True)
        centered = values - row_mean
        row_var = jnp.mean(centered * centered, axis=-1, keepdims=True)
        inverse_std = lax.rsqrt(row_var + norm_eps)
        hat = centered * inverse_std
        scaled = hat * gains + offset
        inverse_len = lax.rsqrt(jnp.sum(scaled * scaled, axis=-1, keepdims=True) + unit_eps)
        unit = scaled * inverse_len
        along = unit * gains
        mean_along = jnp.mean(along, axis=-1, keepdims=True)
        mean_along_hat = jnp.mean(along * hat, axis=-1, keepdims=True)
        unit_ref[tower] = (unit * carry_scale).astype(jnp.bfloat16)
        rows_ref[tower, :, :width] = acts
        lane = lax.broadcasted_iota(jnp.int32, (acts.shape[0], lanes), 1)
        record = jnp.zeros((acts.shape[0], lanes), jnp.float32)
        index = 0
        for stat in (row_mean, inverse_std, inverse_len, mean_along, mean_along_hat):
            for part in split_three(stat):
                record = jnp.where(lane == index, part, record)
                index += 1
        rows_ref[tower, :, width:] = record.astype(jnp.bfloat16)


def prepare(image_acts, text_acts, *vectors):
    rows, width = image_acts.shape
    return pl.pallas_call(
        prepare_kernel,
        out_shape=(
            jax.ShapeDtypeStruct((2, rows, width), jnp.bfloat16),
            jax.ShapeDtypeStruct((2, rows, width + lanes), jnp.bfloat16),
        ),
    )(image_acts, text_acts, *vectors)


def pair_kernel(
    place_ref,
    fixed_ref,
    ig_ref,
    io_ref,
    tg_ref,
    to_ref,
    moving_ref,
    out_ref,
    embed,
    probs,
    part,
):
    blocks, towers, group, _ = fixed_ref.shape
    columns, width = moving_ref.shape[1:]
    per_block = block_rows // group
    rate = logit_scale * log2_e / carry_scale
    shift = -logit_shift * log2_e
    vectors = ((ig_ref, io_ref), (tg_ref, to_ref))
    my_row, my_block = place_ref[0], place_ref[1]
    window = lanes // group
    pair_row = my_row // window

    def probability(scores):
        return 1.0 / (1.0 + jnp.exp2(shift - rate * scores))

    def stats_of(block, tower, start):
        record = fixed_ref[block, tower, start : start + chunk_rows, width:].astype(jnp.float32)
        return [
            record[:, 3 * k : 3 * k + 1]
            + (record[:, 3 * k + 1 : 3 * k + 2] + record[:, 3 * k + 2 : 3 * k + 3])
            for k in range(5)
        ]

    def forward(slot, tower, first):
        gains = vectors[tower][0][...].reshape(1, width)
        offset = vectors[tower][1][...].reshape(1, width)
        for index in range(per_block):
            for start in range(0, group, chunk_rows):
                mean, std, length, _, _ = stats_of(first + index, tower, start)
                acts = fixed_ref[first + index, tower, start : start + chunk_rows, :width]
                hat = (acts.astype(jnp.float32) - mean) * std
                unit = (hat * gains + offset) * length
                at = index * group + start
                embed[slot, at : at + chunk_rows] = unit.astype(jnp.bfloat16)

    def score(slot, tower):
        moving = moving_ref[1 - tower]
        fixed = embed[slot]
        scores = lax.dot_general(fixed, moving, last_last, preferred_element_type=jnp.float32)
        probs[slot] = probability(scores).astype(jnp.bfloat16)

    def label(slot, tower, first):
        mine = my_block - first

        @pl.when(jnp.logical_and(mine >= 0, mine < per_block))
        def _():
            rows = pl.ds(pl.multiple_of(mine * group, group), group)
            cols = pl.ds(pl.multiple_of(pair_row * lanes, lanes), lanes)
            scores = lax.dot_general(
                embed[slot, rows],
                moving_ref[1 - tower, cols],
                last_last,
                preferred_element_type=jnp.float32,
            )
            row_index = lax.broadcasted_iota(jnp.int32, scores.shape, 0)
            col_index = lax.broadcasted_iota(jnp.int32, scores.shape, 1)
            own = row_index == col_index - (my_row % window) * group
            value = probability(scores)
            value = jnp.where(own, value - 1.0, value)
            probs[slot, rows, cols] = value.astype(jnp.bfloat16)

    def gather_grad(slot, tower):
        part[slot] = jnp.dot(probs[slot], moving_ref[1 - tower], preferred_element_type=jnp.float32)

    def backward(slot, tower, first):
        gains = vectors[tower][0][...].reshape(1, width)
        offset = vectors[tower][1][...].reshape(1, width)
        for index in range(per_block):
            for start in range(0, group, chunk_rows):
                at = index * group + start
                mean, std, length, along_one, along_hat = stats_of(first + index, tower, start)
                acts = fixed_ref[first + index, tower, start : start + chunk_rows, :width]
                hat = (acts.astype(jnp.float32) - mean) * std
                grad = part[slot, at : at + chunk_rows]
                weighted = grad * gains
                sum_one = jnp.sum(weighted, axis=-1, keepdims=True)
                sum_hat = jnp.sum(weighted * hat, axis=-1, keepdims=True)
                sum_offset = jnp.sum(grad * offset, axis=-1, keepdims=True)
                along = length * (sum_hat + sum_offset)
                mean_one = sum_one * (1.0 / width) - along * along_one
                mean_two = sum_hat * (1.0 / width) - along * along_hat
                along = along * length
                scale = (logit_scale * loss_weight / carry_scale) * length * std
                removed = (hat * gains + offset) * (gains * along) + hat * mean_two + mean_one
                value = (weighted - removed) * scale
                place = ring_order[first + index]
                out_ref[place, tower, start : start + chunk_rows] = value.astype(jnp.bfloat16)

    jobs = [(t, b) for t in range(towers) for b in range(0, blocks, per_block)]
    for slot, (tower, first) in enumerate(jobs):
        forward(slot, tower, first)
        score(slot, tower)
    for slot, (tower, first) in enumerate(jobs):
        label(slot, tower, first)
    for slot, (tower, first) in enumerate(jobs):
        gather_grad(slot, tower)
        backward(slot, tower, first)


def pair_grads(place, fixed, vectors, moving):
    blocks, towers, group, _ = fixed.shape
    columns, width = moving.shape[1:]
    slots = towers * blocks * group // block_rows
    whole = pl.BlockSpec(memory_space=pltpu.VMEM)
    return pl.pallas_call(
        pair_kernel,
        out_shape=jax.ShapeDtypeStruct((blocks, towers, group, width), jnp.bfloat16),
        in_specs=[pl.BlockSpec(memory_space=pltpu.SMEM)] + [whole] * 6,
        out_specs=whole,
        scratch_shapes=[
            pltpu.VMEM((slots, block_rows, width), jnp.bfloat16),
            pltpu.VMEM((slots, block_rows, columns), jnp.bfloat16),
            pltpu.VMEM((slots, block_rows, width), jnp.float32),
        ],
        compiler_params=pltpu.CompilerParams(vmem_limit_bytes=32 * 1024 * 1024),
        cost_estimate=pl.CostEstimate(
            flops=4 * towers * blocks * group * columns * width,
            bytes_accessed=12 * 1024 * 1024,
            transcendentals=2 * towers * blocks * group * columns,
        ),
    )(place, fixed, *vectors, moving)


def add_kernel(parts_ref, image_ref, text_ref):
    for tower, out_ref in enumerate((image_ref, text_ref)):
        total = parts_ref[0, tower].astype(jnp.float32)
        for block in range(1, parts_ref.shape[0]):
            total = total + parts_ref[block, tower].astype(jnp.float32)
        out_ref[...] = total.astype(jnp.bfloat16)


def add_parts(parts):
    _, _, group, width = parts.shape
    shape = jax.ShapeDtypeStruct((group, width), jnp.bfloat16)
    return pl.pallas_call(add_kernel, out_shape=(shape, shape))(parts)


def body(image_acts, text_acts, image_gain, image_offset, text_gain, text_offset):
    vectors = (image_gain, image_offset, text_gain, text_offset)
    units, rows = prepare(image_acts, text_acts, *vectors)
    fixed = lax.all_gather(rows, "col", axis=0, axis_index_groups=[list(ring_order)])
    moving = lax.all_gather(units.astype(jnp.float16), "row", axis=0)
    moving = jnp.swapaxes(moving, 0, 1).astype(jnp.bfloat16)
    moving = moving.reshape(moving.shape[0], -1, moving.shape[-1])
    col = lax.axis_index("col")
    my_block = jnp.where(col % 2 == 0, col // 2, 7 - col // 2)
    place = jnp.stack([lax.axis_index("row"), my_block]).astype(jnp.int32)
    parts = pair_grads(place, fixed, vectors, moving)
    parts = lax.all_to_all(parts, "col", 0, 0)
    return add_parts(parts)


def solution(mesh):
    placed = (P(("row", "col", "rep"), None), P(("row", "col", "rep"), None), P(), P(), P(), P())
    return jax.shard_map(
        body,
        mesh=mesh,
        in_specs=placed,
        out_specs=(P(("row", "col", "rep"), None), P(("row", "col", "rep"), None)),
        check_vma=False,
    )
```

```python
import functools

import jax
import jax.numpy as jnp
from jax import lax
from jax.experimental import pallas as pl
from jax.experimental.pallas import tpu as pltpu
from jax.sharding import PartitionSpec as P

logit_scale = 10.0
logit_shift = -10.0
loss_weight = 16.0
norm_eps = 1e-06
unit_eps = 1e-06
log2_e = 1.4426950408889634
carry_scale = 32768.0
lanes = 128
chunk_rows = 16
block_rows = 256
stat_count = 5
ring_order = (0, 1, 2, 3, 4, 5, 6, 7)
last_last = (((1,), (1,)), ((), ()))


def split_three(value):
    first = value.astype(jnp.bfloat16)
    rest = value - first.astype(jnp.float32)
    second = rest.astype(jnp.bfloat16)
    third = (rest - second.astype(jnp.float32)).astype(jnp.bfloat16)
    return [part.astype(jnp.float32) for part in (first, second, third)]


def prepare_kernel(image_ref, text_ref, ig_ref, io_ref, tg_ref, to_ref, unit_ref, rows_ref):
    width = image_ref.shape[1]
    sides = ((image_ref, ig_ref, io_ref), (text_ref, tg_ref, to_ref))
    for tower, (acts_ref, gain_ref, offset_ref) in enumerate(sides):
        acts = acts_ref[...]
        gains = gain_ref[...].reshape(1, width)
        offset = offset_ref[...].reshape(1, width)
        values = acts.astype(jnp.float32)
        row_mean = jnp.mean(values, axis=-1, keepdims=True)
        centered = values - row_mean
        row_var = jnp.mean(centered * centered, axis=-1, keepdims=True)
        inverse_std = lax.rsqrt(row_var + norm_eps)
        hat = centered * inverse_std
        scaled = hat * gains + offset
        inverse_len = lax.rsqrt(jnp.sum(scaled * scaled, axis=-1, keepdims=True) + unit_eps)
        unit = scaled * inverse_len
        along = unit * gains
        mean_along = jnp.mean(along, axis=-1, keepdims=True)
        mean_along_hat = jnp.mean(along * hat, axis=-1, keepdims=True)
        unit_ref[tower] = (unit * carry_scale).astype(jnp.bfloat16)
        for copy in range(rows_ref.shape[0]):
            rows_ref[copy, tower, :, :width] = acts
        lane = lax.broadcasted_iota(jnp.int32, (acts.shape[0], lanes), 1)
        record = jnp.zeros((acts.shape[0], lanes), jnp.float32)
        index = 0
        for stat in (row_mean, inverse_std, inverse_len, mean_along, mean_along_hat):
            for part in split_three(stat):
                record = jnp.where(lane == index, part, record)
                index += 1
        record = record.astype(jnp.bfloat16)
        for copy in range(rows_ref.shape[0]):
            rows_ref[copy, tower, :, width:] = record


def prepare(copies, image_acts, text_acts, *vectors):
    rows, width = image_acts.shape
    return pl.pallas_call(
        prepare_kernel,
        out_shape=(
            jax.ShapeDtypeStruct((2, rows, width), jnp.bfloat16),
            jax.ShapeDtypeStruct((copies, 2, rows, width + lanes), jnp.bfloat16),
        ),
    )(image_acts, text_acts, *vectors)


def pair_kernel(
    place_ref,
    fixed_ref,
    ig_ref,
    io_ref,
    tg_ref,
    to_ref,
    moving_hbm,
    out_ref,
    moving_ref,
    arrived,
    stats,
    embed,
    probs,
    part,
):
    blocks, towers, group, _ = fixed_ref.shape
    _, planes, _, width = moving_ref.shape
    columns = planes * group
    per_block = block_rows // group
    rate = logit_scale * log2_e / carry_scale
    shift = -logit_shift * log2_e
    copies = [
        pltpu.make_async_copy(moving_hbm.at[:, t], moving_ref.at[t], arrived.at[t])
        for t in range(towers)
    ]
    for copy in reversed(copies):
        copy.start()
    vectors = ((ig_ref, io_ref), (tg_ref, to_ref))
    my_row, my_block = place_ref[0], place_ref[1]
    window = lanes // group
    pair_row = my_row // window
    spread_rows = lax.broadcasted_iota(jnp.int32, (lanes, stat_count * lanes), 0)
    spread_cols = lax.broadcasted_iota(jnp.int32, (lanes, stat_count * lanes), 1)
    spread = spread_rows // 3 == spread_cols // lanes
    spread = jnp.where(spread, jnp.float32(1.0), jnp.float32(0.0)).astype(jnp.bfloat16)

    def probability(scores):
        return 1.0 / (1.0 + jnp.exp2(shift - rate * scores))

    def moving_rows(tower):
        return moving_ref[1 - tower].reshape(columns, width)

    def wide(value):
        return jnp.concatenate([value] * (width // lanes), axis=1)

    def chunks(first):
        for index in range(per_block):
            for start in range(0, group, chunk_rows):
                yield first + index, start, index * group + start

    def stat(slot, at, which):
        return stats[slot, at : at + chunk_rows, which * lanes : (which + 1) * lanes]

    def hat_rows(slot, tower, block, start, at):
        acts = fixed_ref[block, tower, start : start + chunk_rows, :width].astype(jnp.float32)
        return (acts - wide(stat(slot, at, 0))) * wide(stat(slot, at, 1))

    def forward(slot, tower, first):
        gains = vectors[tower][0][...].reshape(1, width)
        offset = vectors[tower][1][...].reshape(1, width)
        record = fixed_ref[first : first + per_block, tower, :, width:].reshape(block_rows, lanes)
        stats[slot] = jnp.dot(record, spread, preferred_element_type=jnp.float32)
        for block, start, at in chunks(first):
            hat = hat_rows(slot, tower, block, start, at)
            unit = (hat * gains + offset) * wide(stat(slot, at, 2))
            embed[slot, at : at + chunk_rows] = unit.astype(jnp.bfloat16)

    def score(slot, tower):
        scores = lax.dot_general(
            embed[slot], moving_rows(tower), last_last, preferred_element_type=jnp.float32
        )
        probs[slot] = probability(scores).astype(jnp.bfloat16)

    def label(tower):
        slot = tower * (blocks // per_block) + my_block // per_block
        start = (my_block % per_block) * group
        rows = pl.ds(pl.multiple_of(start, group), group)
        cols = pl.ds(pl.multiple_of(pair_row * lanes, lanes), lanes)
        near = moving_ref[1 - tower, pl.ds(pair_row * window, window)].reshape(lanes, width)
        scores = lax.dot_general(
            embed[slot, rows], near, last_last, preferred_element_type=jnp.float32
        )
        row_index = lax.broadcasted_iota(jnp.int32, scores.shape, 0)
        col_index = lax.broadcasted_iota(jnp.int32, scores.shape, 1)
        own = row_index == col_index - (my_row % window) * group
        value = probability(scores)
        value = jnp.where(own, value - 1.0, value)
        probs[slot, rows, cols] = value.astype(jnp.bfloat16)

    def collect(slot, tower):
        part[slot] = jnp.dot(probs[slot], moving_rows(tower), preferred_element_type=jnp.float32)

    def backward(slot, tower, first):
        gains = vectors[tower][0][...].reshape(1, width)
        offset = vectors[tower][1][...].reshape(1, width)
        gains_two = gains * gains
        gains_offset = gains * offset
        for block, start, at in chunks(first):
            hat = hat_rows(slot, tower, block, start, at)
            grad = part[slot, at : at + chunk_rows]
            weighted = grad * gains
            sum_one = jnp.sum(weighted, axis=-1, keepdims=True)
            sum_hat = jnp.sum(weighted * hat, axis=-1, keepdims=True)
            sum_offset = jnp.sum(grad * offset, axis=-1, keepdims=True)
            length = stat(slot, at, 2)
            along = length * (sum_hat + sum_offset)
            mean_one = sum_one * (1.0 / width) - along * stat(slot, at, 3)
            mean_two = sum_hat * (1.0 / width) - along * stat(slot, at, 4)
            along = wide(along * length)
            scale = (logit_scale * loss_weight / carry_scale) * length * stat(slot, at, 1)
            removed = hat * (gains_two * along + wide(mean_two))
            removed = removed + (gains_offset * along + wide(mean_one))
            value = (weighted - removed) * wide(scale)
            out_ref[ring_order[block], tower, start : start + chunk_rows] = value.astype(
                jnp.bfloat16
            )

    jobs = [(t, b) for t in range(towers) for b in range(0, blocks, per_block)]
    for slot, (tower, first) in enumerate(jobs):
        forward(slot, tower, first)
    for slot, (tower, first) in enumerate(jobs):
        if first == 0:
            copies[1 - tower].wait()
        score(slot, tower)
    for tower in range(towers):
        label(tower)
    for slot, (tower, first) in enumerate(jobs):
        collect(slot, tower)
        backward(slot, tower, first)


def pair_grads(place, fixed, vectors, moving):
    blocks, towers, group, _ = fixed.shape
    planes, _, _, width = moving.shape
    columns = planes * group
    slots = towers * blocks * group // block_rows
    whole = pl.BlockSpec(memory_space=pltpu.VMEM)
    return pl.pallas_call(
        pair_kernel,
        out_shape=jax.ShapeDtypeStruct((blocks, towers, group, width), jnp.bfloat16),
        in_specs=[pl.BlockSpec(memory_space=pltpu.SMEM)]
        + [whole] * 5
        + [pl.BlockSpec(memory_space=pl.ANY)],
        out_specs=whole,
        scratch_shapes=[
            pltpu.VMEM((towers, planes, group, width), jnp.bfloat16),
            pltpu.SemaphoreType.DMA((towers,)),
            pltpu.VMEM((slots, block_rows, stat_count * lanes), jnp.float32),
            pltpu.VMEM((slots, block_rows, width), jnp.bfloat16),
            pltpu.VMEM((slots, block_rows, columns), jnp.bfloat16),
            pltpu.VMEM((slots, block_rows, width), jnp.float32),
        ],
        compiler_params=pltpu.CompilerParams(vmem_limit_bytes=24 * 1024 * 1024),
        cost_estimate=pl.CostEstimate(
            flops=4 * towers * blocks * group * columns * width,
            bytes_accessed=12 * 1024 * 1024,
            transcendentals=2 * towers * blocks * group * columns,
        ),
    )(place, fixed, *vectors, moving)


def add_kernel(parts_ref, image_ref, text_ref):
    for tower, out_ref in enumerate((image_ref, text_ref)):
        total = parts_ref[0, tower].astype(jnp.float32)
        for block in range(1, parts_ref.shape[0]):
            total = total + parts_ref[block, tower].astype(jnp.float32)
        out_ref[...] = total.astype(jnp.bfloat16)


def add_parts(parts):
    _, _, group, width = parts.shape
    shape = jax.ShapeDtypeStruct((group, width), jnp.bfloat16)
    return pl.pallas_call(add_kernel, out_shape=(shape, shape))(parts)


def body(image_acts, text_acts, image_gain, image_offset, text_gain, text_offset):
    vectors = (image_gain, image_offset, text_gain, text_offset)
    units, copies = prepare(lax.axis_size("col"), image_acts, text_acts, *vectors)
    fixed = lax.all_to_all(copies, "col", 0, 0)
    moving = lax.all_gather(units.astype(jnp.float16), "row", axis=0)
    moving = moving.astype(jnp.bfloat16)
    col = lax.axis_index("col")
    my_block = col
    place = jnp.stack([lax.axis_index("row"), my_block]).astype(jnp.int32)
    moving = pltpu.with_memory_space_constraint(moving, pltpu.HBM)
    parts = pair_grads(place, fixed, vectors, moving)
    parts = lax.all_to_all(parts, "col", 0, 0)
    grads = []
    for tower in range(parts.shape[1]):
        total = parts[0, tower].astype(jnp.float32)
        for block in range(1, parts.shape[0]):
            total = total + parts[block, tower].astype(jnp.float32)
        grads.append(total.astype(jnp.bfloat16))
    return tuple(grads)


def solution(mesh):
    placed = (P(("row", "col", "rep"), None), P(("row", "col", "rep"), None), P(), P(), P(), P())
    return jax.shard_map(
        body,
        mesh=mesh,
        in_specs=placed,
        out_specs=(P(("row", "col", "rep"), None), P(("row", "col", "rep"), None)),
        check_vma=False,
    )
```

```python
import functools

import jax
import jax.numpy as jnp
from jax import lax
from jax.experimental import pallas as pl
from jax.experimental.pallas import tpu as pltpu
from jax.sharding import PartitionSpec as P

logit_scale = 10.0
logit_shift = -10.0
loss_weight = 16.0
norm_eps = 1e-06
unit_eps = 1e-06
log2_e = 1.4426950408889634
carry_scale = 32768.0
lanes = 128
chunk_rows = 16
block_rows = 256
stat_count = 5
ring_order = (0, 1, 2, 3, 4, 5, 6, 7)
last_last = (((1,), (1,)), ((), ()))


def split_three(value):
    first = value.astype(jnp.bfloat16)
    rest = value - first.astype(jnp.float32)
    second = rest.astype(jnp.bfloat16)
    third = (rest - second.astype(jnp.float32)).astype(jnp.bfloat16)
    return [part.astype(jnp.float32) for part in (first, second, third)]


def prepare_kernel(image_ref, text_ref, ig_ref, io_ref, tg_ref, to_ref, unit_ref, rows_ref):
    width = image_ref.shape[1]
    is_image = pl.program_id(0) == 0
    acts = jnp.where(is_image, image_ref[...], text_ref[...])
    gains = jnp.where(is_image, ig_ref[...], tg_ref[...]).reshape(1, width)
    offset = jnp.where(is_image, io_ref[...], to_ref[...]).reshape(1, width)
    values = acts.astype(jnp.float32)
    row_mean = jnp.mean(values, axis=-1, keepdims=True)
    centered = values - row_mean
    row_var = jnp.mean(centered * centered, axis=-1, keepdims=True)
    inverse_std = lax.rsqrt(row_var + norm_eps)
    hat = centered * inverse_std
    scaled = hat * gains + offset
    inverse_len = lax.rsqrt(jnp.sum(scaled * scaled, axis=-1, keepdims=True) + unit_eps)
    unit = scaled * inverse_len
    along = unit * gains
    mean_along = jnp.mean(along, axis=-1, keepdims=True)
    mean_along_hat = jnp.mean(along * hat, axis=-1, keepdims=True)
    unit_ref[...] = (unit * carry_scale).astype(jnp.bfloat16)
    lane = lax.broadcasted_iota(jnp.int32, (acts.shape[0], lanes), 1)
    record = jnp.zeros((acts.shape[0], lanes), jnp.float32)
    index = 0
    for stat in (row_mean, inverse_std, inverse_len, mean_along, mean_along_hat):
        for part in split_three(stat):
            record = jnp.where(lane == index, part, record)
            index += 1
    record = record.astype(jnp.bfloat16)
    for copy in range(rows_ref.shape[0]):
        rows_ref[copy, :, :width] = acts
        rows_ref[copy, :, width:] = record


def prepare(copies, image_acts, text_acts, *vectors):
    rows, width = image_acts.shape
    acts_spec = pl.BlockSpec((rows, width), lambda t: (0, 0))
    vector = pl.BlockSpec((width,), lambda t: (0,))
    return pl.pallas_call(
        prepare_kernel,
        grid=(2,),
        out_shape=(
            jax.ShapeDtypeStruct((2, rows, width), jnp.bfloat16),
            jax.ShapeDtypeStruct((copies, 2, rows, width + lanes), jnp.bfloat16),
        ),
        in_specs=[acts_spec, acts_spec, vector, vector, vector, vector],
        out_specs=(
            pl.BlockSpec((None, rows, width), lambda t: (t, 0, 0)),
            pl.BlockSpec((copies, None, rows, width + lanes), lambda t: (0, t, 0, 0)),
        ),
    )(image_acts, text_acts, *vectors)


def pair_kernel(
    place_ref,
    fixed_ref,
    ig_ref,
    io_ref,
    tg_ref,
    to_ref,
    moving_hbm,
    out_ref,
    moving_ref,
    arrived,
    stats,
    embed,
    probs,
    part,
):
    blocks, towers, group, _ = fixed_ref.shape
    _, planes, _, width = moving_ref.shape
    columns = planes * group
    per_block = block_rows // group
    rate = logit_scale * log2_e / carry_scale
    shift = -logit_shift * log2_e
    copies = [
        pltpu.make_async_copy(moving_hbm.at[:, t], moving_ref.at[t], arrived.at[t])
        for t in range(towers)
    ]
    for copy in reversed(copies):
        copy.start()
    vectors = ((ig_ref, io_ref), (tg_ref, to_ref))
    my_row, my_block = place_ref[0], place_ref[1]
    spread_rows = lax.broadcasted_iota(jnp.int32, (lanes, stat_count * lanes), 0)
    spread_cols = lax.broadcasted_iota(jnp.int32, (lanes, stat_count * lanes), 1)
    spread = spread_rows // 3 == spread_cols // lanes
    spread = jnp.where(spread, jnp.float32(1.0), jnp.float32(0.0)).astype(jnp.bfloat16)

    def probability(scores):
        return 1.0 / (1.0 + jnp.exp2(shift - rate * scores))

    def moving_rows(tower):
        return moving_ref[1 - tower].reshape(columns, width)

    def wide(value):
        return jnp.concatenate([value] * (width // lanes), axis=1)

    def chunks(first):
        for index in range(per_block):
            for start in range(0, group, chunk_rows):
                yield first + index, start, index * group + start

    def stat(slot, at, which):
        return stats[slot, at : at + chunk_rows, which * lanes : (which + 1) * lanes]

    def hat_rows(slot, tower, block, start, at):
        acts = fixed_ref[block, tower, start : start + chunk_rows, :width].astype(jnp.float32)
        return (acts - wide(stat(slot, at, 0))) * wide(stat(slot, at, 1))

    def forward(slot, tower, first):
        gains = vectors[tower][0][...].reshape(1, width)
        offset = vectors[tower][1][...].reshape(1, width)
        record = fixed_ref[first : first + per_block, tower, :, width:].reshape(block_rows, lanes)
        stats[slot] = jnp.dot(record, spread, preferred_element_type=jnp.float32)
        for block, start, at in chunks(first):
            hat = hat_rows(slot, tower, block, start, at)
            unit = (hat * gains + offset) * wide(stat(slot, at, 2))
            embed[slot, at : at + chunk_rows] = unit.astype(jnp.bfloat16)

    def score(slot, tower, first):
        scores = lax.dot_general(
            embed[slot], moving_rows(tower), last_last, preferred_element_type=jnp.float32
        )
        row_index = lax.broadcasted_iota(jnp.int32, scores.shape, 0) + (first - my_block) * group
        col_index = lax.broadcasted_iota(jnp.int32, scores.shape, 1) - my_row * group
        inside = jnp.logical_and(col_index >= 0, col_index < group)
        col_index = jnp.where(inside, col_index, -1 - block_rows * blocks)
        value = probability(scores)
        value = jnp.where(row_index == col_index, value - 1.0, value)
        probs[slot] = value.astype(jnp.bfloat16)

    def collect(slot, tower):
        part[slot] = jnp.dot(probs[slot], moving_rows(tower), preferred_element_type=jnp.float32)

    def backward(slot, tower, first):
        gains = vectors[tower][0][...].reshape(1, width)
        offset = vectors[tower][1][...].reshape(1, width)
        gains_two = gains * gains
        gains_offset = gains * offset
        for block, start, at in chunks(first):
            acts = fixed_ref[block, tower, start : start + chunk_rows, :width]
            centered = acts.astype(jnp.float32) - wide(stat(slot, at, 0))
            grad = part[slot, at : at + chunk_rows]
            weighted = grad * gains
            std, length = stat(slot, at, 1), stat(slot, at, 2)
            sum_one = jnp.sum(weighted, axis=-1, keepdims=True)
            sum_hat = std * jnp.sum(weighted * centered, axis=-1, keepdims=True)
            sum_offset = jnp.sum(grad * offset, axis=-1, keepdims=True)
            along = length * (sum_hat + sum_offset)
            mean_one = sum_one * (1.0 / width) - along * stat(slot, at, 3)
            mean_two = sum_hat * (1.0 / width) - along * stat(slot, at, 4)
            along = along * length
            scale = (logit_scale * loss_weight / carry_scale) * length * std
            removed = centered * (gains_two * wide(along * std) + wide(mean_two * std))
            removed = removed + (gains_offset * wide(along) + wide(mean_one))
            value = (weighted - removed) * wide(scale)
            out_ref[ring_order[block], tower, start : start + chunk_rows] = value.astype(
                jnp.bfloat16
            )

    jobs = [(t, b) for t in range(towers) for b in range(0, blocks, per_block)]
    for slot, (tower, first) in enumerate(jobs):
        forward(slot, tower, first)
    for slot, (tower, first) in enumerate(jobs):
        if first == 0:
            copies[1 - tower].wait()
        score(slot, tower, first)
        collect(slot, tower)
        backward(slot, tower, first)


def pair_grads(place, fixed, vectors, moving):
    blocks, towers, group, _ = fixed.shape
    planes, _, _, width = moving.shape
    columns = planes * group
    slots = towers * blocks * group // block_rows
    whole = pl.BlockSpec(memory_space=pltpu.VMEM)
    return pl.pallas_call(
        pair_kernel,
        out_shape=jax.ShapeDtypeStruct((blocks, towers, group, width), jnp.bfloat16),
        in_specs=[pl.BlockSpec(memory_space=pltpu.SMEM)]
        + [whole] * 5
        + [pl.BlockSpec(memory_space=pl.ANY)],
        out_specs=whole,
        scratch_shapes=[
            pltpu.VMEM((towers, planes, group, width), jnp.bfloat16),
            pltpu.SemaphoreType.DMA((towers,)),
            pltpu.VMEM((slots, block_rows, stat_count * lanes), jnp.float32),
            pltpu.VMEM((slots, block_rows, width), jnp.bfloat16),
            pltpu.VMEM((slots, block_rows, columns), jnp.bfloat16),
            pltpu.VMEM((slots, block_rows, width), jnp.float32),
        ],
        compiler_params=pltpu.CompilerParams(vmem_limit_bytes=24 * 1024 * 1024),
        cost_estimate=pl.CostEstimate(
            flops=4 * towers * blocks * group * columns * width,
            bytes_accessed=12 * 1024 * 1024,
            transcendentals=2 * towers * blocks * group * columns,
        ),
    )(place, fixed, *vectors, moving)


def add_kernel(parts_ref, image_ref, text_ref):
    for tower, out_ref in enumerate((image_ref, text_ref)):
        total = parts_ref[0, tower].astype(jnp.float32)
        for block in range(1, parts_ref.shape[0]):
            total = total + parts_ref[block, tower].astype(jnp.float32)
        out_ref[...] = total.astype(jnp.bfloat16)


def add_parts(parts):
    _, _, group, width = parts.shape
    shape = jax.ShapeDtypeStruct((group, width), jnp.bfloat16)
    return pl.pallas_call(add_kernel, out_shape=(shape, shape))(parts)


def body(image_acts, text_acts, image_gain, image_offset, text_gain, text_offset):
    vectors = (image_gain, image_offset, text_gain, text_offset)
    units, copies = prepare(lax.axis_size("col"), image_acts, text_acts, *vectors)
    fixed = lax.all_to_all(copies, "col", 0, 0)
    moving = lax.all_gather(units.astype(jnp.float16), "row", axis=0)
    moving = moving.astype(jnp.bfloat16)
    col = lax.axis_index("col")
    my_block = col
    place = jnp.stack([lax.axis_index("row"), my_block]).astype(jnp.int32)
    moving = pltpu.with_memory_space_constraint(moving, pltpu.HBM)
    parts = pair_grads(place, fixed, vectors, moving)
    parts = lax.all_to_all(parts, "col", 0, 0)
    grads = []
    for tower in range(parts.shape[1]):
        total = parts[0, tower].astype(jnp.float32)
        for block in range(1, parts.shape[0]):
            total = total + parts[block, tower].astype(jnp.float32)
        grads.append(total.astype(jnp.bfloat16))
    return tuple(grads)


def solution(mesh):
    placed = (P(("row", "col", "rep"), None), P(("row", "col", "rep"), None), P(), P(), P(), P())
    return jax.shard_map(
        body,
        mesh=mesh,
        in_specs=placed,
        out_specs=(P(("row", "col", "rep"), None), P(("row", "col", "rep"), None)),
        check_vma=False,
    )
```

```python
import functools

import jax
import jax.numpy as jnp
from jax import lax
from jax.experimental import pallas as pl
from jax.experimental.pallas import tpu as pltpu
from jax.sharding import PartitionSpec as P

logit_scale = 10.0
logit_shift = -10.0
loss_weight = 16.0
norm_eps = 1e-06
unit_eps = 1e-06
log2_e = 1.4426950408889634
carry_scale = 32768.0
lanes = 128
chunk_rows = 16
block_rows = 256
stat_count = 5
ring_order = (0, 1, 2, 3, 4, 5, 6, 7)
last_last = (((1,), (1,)), ((), ()))


def split_three(value):
    first = value.astype(jnp.bfloat16)
    rest = value - first.astype(jnp.float32)
    second = rest.astype(jnp.bfloat16)
    third = (rest - second.astype(jnp.float32)).astype(jnp.bfloat16)
    return [part.astype(jnp.float32) for part in (first, second, third)]


def prepare_kernel(image_ref, text_ref, ig_ref, io_ref, tg_ref, to_ref, unit_ref, rows_ref):
    width = image_ref.shape[1]
    is_image = pl.program_id(0) == 0
    acts = jnp.where(is_image, image_ref[...], text_ref[...])
    gains = jnp.where(is_image, ig_ref[...], tg_ref[...]).reshape(1, width)
    offset = jnp.where(is_image, io_ref[...], to_ref[...]).reshape(1, width)
    values = acts.astype(jnp.float32)
    row_mean = jnp.mean(values, axis=-1, keepdims=True)
    centered = values - row_mean
    row_var = jnp.mean(centered * centered, axis=-1, keepdims=True)
    inverse_std = lax.rsqrt(row_var + norm_eps)
    hat = centered * inverse_std
    scaled = hat * gains + offset
    inverse_len = lax.rsqrt(jnp.sum(scaled * scaled, axis=-1, keepdims=True) + unit_eps)
    unit = scaled * inverse_len
    along = unit * gains
    mean_along = jnp.mean(along, axis=-1, keepdims=True)
    mean_along_hat = jnp.mean(along * hat, axis=-1, keepdims=True)
    unit_ref[...] = (unit * carry_scale).astype(jnp.bfloat16)
    lane = lax.broadcasted_iota(jnp.int32, (acts.shape[0], lanes), 1)
    record = jnp.zeros((acts.shape[0], lanes), jnp.float32)
    index = 0
    for stat in (row_mean, inverse_std, inverse_len, mean_along, mean_along_hat):
        for part in split_three(stat):
            record = jnp.where(lane == index, part, record)
            index += 1
    record = record.astype(jnp.bfloat16)
    for copy in range(rows_ref.shape[0]):
        rows_ref[copy, :, :width] = acts
        rows_ref[copy, :, width:] = record


def prepare(copies, image_acts, text_acts, *vectors):
    rows, width = image_acts.shape
    acts_spec = pl.BlockSpec((rows, width), lambda t: (0, 0))
    vector = pl.BlockSpec((width,), lambda t: (0,))
    return pl.pallas_call(
        prepare_kernel,
        grid=(2,),
        out_shape=(
            pltpu.VMEM((2, rows, width), jnp.bfloat16),
            jax.ShapeDtypeStruct((copies, 2, rows, width + lanes), jnp.bfloat16),
        ),
        in_specs=[acts_spec, acts_spec, vector, vector, vector, vector],
        out_specs=(
            pl.BlockSpec((None, rows, width), lambda t: (t, 0, 0)),
            pl.BlockSpec((copies, None, rows, width + lanes), lambda t: (0, t, 0, 0)),
        ),
    )(image_acts, text_acts, *vectors)


def pair_kernel(
    place_ref,
    fixed_ref,
    ig_ref,
    io_ref,
    tg_ref,
    to_ref,
    moving_hbm,
    out_ref,
    moving_ref,
    arrived,
    stats,
    embed,
    probs,
    part,
):
    blocks, towers, group, _ = fixed_ref.shape
    _, planes, _, width = moving_ref.shape
    columns = planes * group
    per_block = block_rows // group
    rate = logit_scale * log2_e / carry_scale
    shift = -logit_shift * log2_e
    copies = [
        pltpu.make_async_copy(moving_hbm.at[t], moving_ref.at[t], arrived.at[t])
        for t in range(towers)
    ]
    for copy in reversed(copies):
        copy.start()
    vectors = ((ig_ref, io_ref), (tg_ref, to_ref))
    my_row, my_block = place_ref[0], place_ref[1]
    spread_rows = lax.broadcasted_iota(jnp.int32, (lanes, stat_count * lanes), 0)
    spread_cols = lax.broadcasted_iota(jnp.int32, (lanes, stat_count * lanes), 1)
    spread = spread_rows // 3 == spread_cols // lanes
    spread = jnp.where(spread, jnp.float32(1.0), jnp.float32(0.0)).astype(jnp.bfloat16)

    def probability(scores):
        return 1.0 / (1.0 + jnp.exp2(shift - rate * scores))

    def moving_rows(tower):
        return moving_ref[1 - tower].reshape(columns, width)

    def wide(value):
        return jnp.concatenate([value] * (width // lanes), axis=1)

    def chunks(first):
        for index in range(per_block):
            for start in range(0, group, chunk_rows):
                yield first + index, start, index * group + start

    def stat(slot, at, which):
        return stats[slot, at : at + chunk_rows, which * lanes : (which + 1) * lanes]

    def hat_rows(slot, tower, block, start, at):
        acts = fixed_ref[block, tower, start : start + chunk_rows, :width].astype(jnp.float32)
        return (acts - wide(stat(slot, at, 0))) * wide(stat(slot, at, 1))

    def forward(slot, tower, first):
        gains = vectors[tower][0][...].reshape(1, width)
        offset = vectors[tower][1][...].reshape(1, width)
        record = fixed_ref[first : first + per_block, tower, :, width:].reshape(block_rows, lanes)
        stats[slot] = jnp.dot(record, spread, preferred_element_type=jnp.float32)
        for block, start, at in chunks(first):
            hat = hat_rows(slot, tower, block, start, at)
            unit = (hat * gains + offset) * wide(stat(slot, at, 2))
            embed[slot, at : at + chunk_rows] = unit.astype(jnp.bfloat16)

    def score(slot, tower, first):
        scores = lax.dot_general(
            embed[slot], moving_rows(tower), last_last, preferred_element_type=jnp.float32
        )
        row_index = lax.broadcasted_iota(jnp.int32, scores.shape, 0) + (first - my_block) * group
        col_index = lax.broadcasted_iota(jnp.int32, scores.shape, 1) - my_row * group
        inside = jnp.logical_and(col_index >= 0, col_index < group)
        col_index = jnp.where(inside, col_index, -1 - block_rows * blocks)
        value = probability(scores)
        value = jnp.where(row_index == col_index, value - 1.0, value)
        probs[slot] = value.astype(jnp.bfloat16)

    def collect(slot, tower):
        part[slot] = jnp.dot(probs[slot], moving_rows(tower), preferred_element_type=jnp.float32)

    def backward(slot, tower, first):
        gains = vectors[tower][0][...].reshape(1, width)
        offset = vectors[tower][1][...].reshape(1, width)
        gains_two = gains * gains
        gains_offset = gains * offset
        for block, start, at in chunks(first):
            acts = fixed_ref[block, tower, start : start + chunk_rows, :width]
            centered = acts.astype(jnp.float32) - wide(stat(slot, at, 0))
            grad = part[slot, at : at + chunk_rows]
            weighted = grad * gains
            std, length = stat(slot, at, 1), stat(slot, at, 2)
            sum_one = jnp.sum(weighted, axis=-1, keepdims=True)
            sum_hat = std * jnp.sum(weighted * centered, axis=-1, keepdims=True)
            sum_offset = jnp.sum(grad * offset, axis=-1, keepdims=True)
            along = length * (sum_hat + sum_offset)
            mean_one = sum_one * (1.0 / width) - along * stat(slot, at, 3)
            mean_two = sum_hat * (1.0 / width) - along * stat(slot, at, 4)
            along = along * length
            scale = (logit_scale * loss_weight / carry_scale) * length * std
            removed = centered * (gains_two * wide(along * std) + wide(mean_two * std))
            removed = removed + (gains_offset * wide(along) + wide(mean_one))
            value = (weighted - removed) * wide(scale)
            out_ref[ring_order[block], tower, start : start + chunk_rows] = value.astype(
                jnp.bfloat16
            )

    jobs = [(t, b) for t in range(towers) for b in range(0, blocks, per_block)]
    for slot, (tower, first) in enumerate(jobs):
        forward(slot, tower, first)
    for slot, (tower, first) in enumerate(jobs):
        if first == 0:
            copies[1 - tower].wait()
        score(slot, tower, first)
        collect(slot, tower)
        backward(slot, tower, first)


def pair_grads(place, fixed, vectors, moving):
    blocks, towers, group, _ = fixed.shape
    _, planes, _, width = moving.shape
    columns = planes * group
    slots = towers * blocks * group // block_rows
    whole = pl.BlockSpec(memory_space=pltpu.VMEM)
    return pl.pallas_call(
        pair_kernel,
        out_shape=jax.ShapeDtypeStruct((blocks, towers, group, width), jnp.bfloat16),
        in_specs=[pl.BlockSpec(memory_space=pltpu.SMEM)]
        + [whole] * 5
        + [pl.BlockSpec(memory_space=pl.ANY)],
        out_specs=whole,
        scratch_shapes=[
            pltpu.VMEM((towers, planes, group, width), jnp.bfloat16),
            pltpu.SemaphoreType.DMA((towers,)),
            pltpu.VMEM((slots, block_rows, stat_count * lanes), jnp.float32),
            pltpu.VMEM((slots, block_rows, width), jnp.bfloat16),
            pltpu.VMEM((slots, block_rows, columns), jnp.bfloat16),
            pltpu.VMEM((slots, block_rows, width), jnp.float32),
        ],
        compiler_params=pltpu.CompilerParams(vmem_limit_bytes=24 * 1024 * 1024),
        cost_estimate=pl.CostEstimate(
            flops=4 * towers * blocks * group * columns * width,
            bytes_accessed=12 * 1024 * 1024,
            transcendentals=2 * towers * blocks * group * columns,
        ),
    )(place, fixed, *vectors, moving)


def add_kernel(parts_ref, image_ref, text_ref):
    for tower, out_ref in enumerate((image_ref, text_ref)):
        total = parts_ref[0, tower].astype(jnp.float32)
        for block in range(1, parts_ref.shape[0]):
            total = total + parts_ref[block, tower].astype(jnp.float32)
        out_ref[...] = total.astype(jnp.bfloat16)


def add_parts(parts):
    _, _, group, width = parts.shape
    shape = jax.ShapeDtypeStruct((group, width), jnp.bfloat16)
    return pl.pallas_call(add_kernel, out_shape=(shape, shape))(parts)


def body(image_acts, text_acts, image_gain, image_offset, text_gain, text_offset):
    vectors = (image_gain, image_offset, text_gain, text_offset)
    units, copies = prepare(lax.axis_size("col"), image_acts, text_acts, *vectors)
    fixed = lax.all_to_all(copies, "col", 0, 0)
    moving = lax.all_gather(units.astype(jnp.float16), "row", axis=1)
    moving = moving.astype(jnp.bfloat16)
    col = lax.axis_index("col")
    my_block = col
    place = jnp.stack([lax.axis_index("row"), my_block]).astype(jnp.int32)
    moving = pltpu.with_memory_space_constraint(moving, pltpu.HBM)
    parts = pair_grads(place, fixed, vectors, moving)
    parts = lax.all_to_all(parts, "col", 0, 0)
    grads = []
    for tower in range(parts.shape[1]):
        total = parts[0, tower].astype(jnp.float32)
        for block in range(1, parts.shape[0]):
            total = total + parts[block, tower].astype(jnp.float32)
        grads.append(total.astype(jnp.bfloat16))
    return tuple(grads)


def solution(mesh):
    placed = (P(("row", "col", "rep"), None), P(("row", "col", "rep"), None), P(), P(), P(), P())
    return jax.shard_map(
        body,
        mesh=mesh,
        in_specs=placed,
        out_specs=(P(("row", "col", "rep"), None), P(("row", "col", "rep"), None)),
        check_vma=False,
    )
```

```python
import functools

import jax
import jax.numpy as jnp
from jax import lax
from jax.experimental import pallas as pl
from jax.experimental.pallas import tpu as pltpu
from jax.sharding import PartitionSpec as P

logit_scale = 10.0
logit_shift = -10.0
loss_weight = 16.0
norm_eps = 1e-06
unit_eps = 1e-06
log2_e = 1.4426950408889634
carry_scale = 32768.0
lanes = 128
chunk_rows = 32
block_rows = 256
stat_count = 5
ring_order = (0, 1, 2, 3, 4, 5, 6, 7)
last_last = (((1,), (1,)), ((), ()))


def split_three(value):
    first = value.astype(jnp.bfloat16)
    rest = value - first.astype(jnp.float32)
    second = rest.astype(jnp.bfloat16)
    third = (rest - second.astype(jnp.float32)).astype(jnp.bfloat16)
    return [part.astype(jnp.float32) for part in (first, second, third)]


def prepare_kernel(image_ref, text_ref, ig_ref, io_ref, tg_ref, to_ref, unit_ref, rows_ref):
    width = image_ref.shape[1]
    is_image = pl.program_id(0) == 0
    acts = jnp.where(is_image, image_ref[...], text_ref[...])
    gains = jnp.where(is_image, ig_ref[...], tg_ref[...]).reshape(1, width)
    offset = jnp.where(is_image, io_ref[...], to_ref[...]).reshape(1, width)
    values = acts.astype(jnp.float32)
    row_mean = jnp.mean(values, axis=-1, keepdims=True)
    centered = values - row_mean
    row_var = jnp.mean(centered * centered, axis=-1, keepdims=True)
    inverse_std = lax.rsqrt(row_var + norm_eps)
    hat = centered * inverse_std
    scaled = hat * gains + offset
    inverse_len = lax.rsqrt(jnp.sum(scaled * scaled, axis=-1, keepdims=True) + unit_eps)
    unit = scaled * inverse_len
    along = unit * gains
    mean_along = jnp.mean(along, axis=-1, keepdims=True)
    mean_along_hat = jnp.mean(along * hat, axis=-1, keepdims=True)
    unit_ref[...] = (unit * carry_scale).astype(jnp.bfloat16)
    lane = lax.broadcasted_iota(jnp.int32, (acts.shape[0], lanes), 1)
    record = jnp.zeros((acts.shape[0], lanes), jnp.float32)
    index = 0
    for stat in (row_mean, inverse_std, inverse_len, mean_along, mean_along_hat):
        for part in split_three(stat):
            record = jnp.where(lane == index, part, record)
            index += 1
    record = record.astype(jnp.bfloat16)
    for copy in range(rows_ref.shape[0]):
        rows_ref[copy, :, :width] = acts
        rows_ref[copy, :, width:] = record


def prepare(copies, image_acts, text_acts, *vectors):
    rows, width = image_acts.shape
    acts_spec = pl.BlockSpec((rows, width), lambda t: (0, 0))
    vector = pl.BlockSpec((width,), lambda t: (0,))
    return pl.pallas_call(
        prepare_kernel,
        grid=(2,),
        out_shape=(
            pltpu.VMEM((2, rows, width), jnp.bfloat16),
            jax.ShapeDtypeStruct((copies, 2, rows, width + lanes), jnp.bfloat16),
        ),
        in_specs=[acts_spec, acts_spec, vector, vector, vector, vector],
        out_specs=(
            pl.BlockSpec((None, rows, width), lambda t: (t, 0, 0)),
            pl.BlockSpec((copies, None, rows, width + lanes), lambda t: (0, t, 0, 0)),
        ),
    )(image_acts, text_acts, *vectors)


def pair_kernel(
    place_ref,
    fixed_ref,
    ig_ref,
    io_ref,
    tg_ref,
    to_ref,
    moving_hbm,
    out_ref,
    moving_ref,
    arrived,
    stats,
    embed,
    probs,
    part,
):
    blocks, towers, group, _ = fixed_ref.shape
    _, planes, _, width = moving_ref.shape
    columns = planes * group
    per_block = block_rows // group
    rate = logit_scale * log2_e / carry_scale
    shift = -logit_shift * log2_e
    copies = [
        pltpu.make_async_copy(moving_hbm.at[t], moving_ref.at[t], arrived.at[t])
        for t in range(towers)
    ]
    for copy in reversed(copies):
        copy.start()
    vectors = ((ig_ref, io_ref), (tg_ref, to_ref))
    my_row, my_block = place_ref[0], place_ref[1]
    spread_rows = lax.broadcasted_iota(jnp.int32, (lanes, stat_count * lanes), 0)
    spread_cols = lax.broadcasted_iota(jnp.int32, (lanes, stat_count * lanes), 1)
    spread = spread_rows // 3 == spread_cols // lanes
    spread = jnp.where(spread, jnp.float32(1.0), jnp.float32(0.0)).astype(jnp.bfloat16)

    def probability(scores):
        return 1.0 / (1.0 + jnp.exp2(shift - rate * scores))

    def moving_rows(tower):
        return moving_ref[1 - tower].reshape(columns, width)

    def wide(value):
        return jnp.concatenate([value] * (width // lanes), axis=1)

    def chunks(first):
        for index in range(per_block):
            for start in range(0, group, chunk_rows):
                yield first + index, start, index * group + start

    def stat(slot, at, which):
        return stats[slot, at : at + chunk_rows, which * lanes : (which + 1) * lanes]

    def hat_rows(slot, tower, block, start, at):
        acts = fixed_ref[block, tower, start : start + chunk_rows, :width].astype(jnp.float32)
        return (acts - wide(stat(slot, at, 0))) * wide(stat(slot, at, 1))

    def forward(slot, tower, first):
        gains = vectors[tower][0][...].reshape(1, width)
        offset = vectors[tower][1][...].reshape(1, width)
        record = fixed_ref[first : first + per_block, tower, :, width:].reshape(block_rows, lanes)
        stats[slot] = jnp.dot(record, spread, preferred_element_type=jnp.float32)
        for block, start, at in chunks(first):
            hat = hat_rows(slot, tower, block, start, at)
            unit = (hat * gains + offset) * wide(stat(slot, at, 2))
            embed[slot, at : at + chunk_rows] = unit.astype(jnp.bfloat16)

    def score(slot, tower, first):
        scores = lax.dot_general(
            embed[slot], moving_rows(tower), last_last, preferred_element_type=jnp.float32
        )
        row_index = lax.broadcasted_iota(jnp.int32, scores.shape, 0) + (first - my_block) * group
        col_index = lax.broadcasted_iota(jnp.int32, scores.shape, 1) - my_row * group
        inside = jnp.logical_and(col_index >= 0, col_index < group)
        col_index = jnp.where(inside, col_index, -1 - block_rows * blocks)
        value = probability(scores)
        value = jnp.where(row_index == col_index, value - 1.0, value)
        probs[slot] = value.astype(jnp.bfloat16)

    def collect(slot, tower):
        part[slot] = jnp.dot(probs[slot], moving_rows(tower), preferred_element_type=jnp.float32)

    def backward(slot, tower, first):
        gains = vectors[tower][0][...].reshape(1, width)
        offset = vectors[tower][1][...].reshape(1, width)
        gains_two = gains * gains
        gains_offset = gains * offset
        for block, start, at in chunks(first):
            acts = fixed_ref[block, tower, start : start + chunk_rows, :width]
            centered = acts.astype(jnp.float32) - wide(stat(slot, at, 0))
            grad = part[slot, at : at + chunk_rows]
            weighted = grad * gains
            std, length = stat(slot, at, 1), stat(slot, at, 2)
            sum_one = jnp.sum(weighted, axis=-1, keepdims=True)
            sum_hat = std * jnp.sum(weighted * centered, axis=-1, keepdims=True)
            sum_offset = jnp.sum(grad * offset, axis=-1, keepdims=True)
            along = length * (sum_hat + sum_offset)
            mean_one = sum_one * (1.0 / width) - along * stat(slot, at, 3)
            mean_two = sum_hat * (1.0 / width) - along * stat(slot, at, 4)
            along = along * length
            scale = (logit_scale * loss_weight / carry_scale) * length * std
            removed = centered * (gains_two * wide(along * std) + wide(mean_two * std))
            removed = removed + (gains_offset * wide(along) + wide(mean_one))
            value = (weighted - removed) * wide(scale)
            out_ref[ring_order[block], tower, start : start + chunk_rows] = value.astype(
                jnp.bfloat16
            )

    jobs = [(t, b) for t in range(towers) for b in range(0, blocks, per_block)]
    for slot, (tower, first) in enumerate(jobs):
        forward(slot, tower, first)
    for slot, (tower, first) in enumerate(jobs):
        if first == 0:
            copies[1 - tower].wait()
        score(slot, tower, first)
        collect(slot, tower)
        backward(slot, tower, first)


def pair_grads(place, fixed, vectors, moving):
    blocks, towers, group, _ = fixed.shape
    _, planes, _, width = moving.shape
    columns = planes * group
    slots = towers * blocks * group // block_rows
    whole = pl.BlockSpec(memory_space=pltpu.VMEM)
    return pl.pallas_call(
        pair_kernel,
        out_shape=jax.ShapeDtypeStruct((blocks, towers, group, width), jnp.bfloat16),
        in_specs=[pl.BlockSpec(memory_space=pltpu.SMEM)]
        + [whole] * 5
        + [pl.BlockSpec(memory_space=pl.ANY)],
        out_specs=whole,
        scratch_shapes=[
            pltpu.VMEM((towers, planes, group, width), jnp.bfloat16),
            pltpu.SemaphoreType.DMA((towers,)),
            pltpu.VMEM((slots, block_rows, stat_count * lanes), jnp.float32),
            pltpu.VMEM((slots, block_rows, width), jnp.bfloat16),
            pltpu.VMEM((slots, block_rows, columns), jnp.bfloat16),
            pltpu.VMEM((slots, block_rows, width), jnp.float32),
        ],
        compiler_params=pltpu.CompilerParams(vmem_limit_bytes=24 * 1024 * 1024),
        cost_estimate=pl.CostEstimate(
            flops=4 * towers * blocks * group * columns * width,
            bytes_accessed=12 * 1024 * 1024,
            transcendentals=2 * towers * blocks * group * columns,
        ),
    )(place, fixed, *vectors, moving)


def add_kernel(parts_ref, image_ref, text_ref):
    for tower, out_ref in enumerate((image_ref, text_ref)):
        total = parts_ref[0, tower].astype(jnp.float32)
        for block in range(1, parts_ref.shape[0]):
            total = total + parts_ref[block, tower].astype(jnp.float32)
        out_ref[...] = total.astype(jnp.bfloat16)


def add_parts(parts):
    _, _, group, width = parts.shape
    shape = jax.ShapeDtypeStruct((group, width), jnp.bfloat16)
    return pl.pallas_call(add_kernel, out_shape=(shape, shape))(parts)


def body(image_acts, text_acts, image_gain, image_offset, text_gain, text_offset):
    vectors = (image_gain, image_offset, text_gain, text_offset)
    units, copies = prepare(lax.axis_size("col"), image_acts, text_acts, *vectors)
    fixed = lax.all_to_all(copies, "col", 0, 0)
    moving = lax.all_gather(units.astype(jnp.float16), "row", axis=1)
    moving = moving.astype(jnp.bfloat16)
    col = lax.axis_index("col")
    my_block = col
    place = jnp.stack([lax.axis_index("row"), my_block]).astype(jnp.int32)
    moving = pltpu.with_memory_space_constraint(moving, pltpu.HBM)
    parts = pair_grads(place, fixed, vectors, moving)
    parts = lax.all_to_all(parts, "col", 0, 0)
    grads = []
    for tower in range(parts.shape[1]):
        total = parts[0, tower].astype(jnp.float32)
        for block in range(1, parts.shape[0]):
            total = total + parts[block, tower].astype(jnp.float32)
        grads.append(total.astype(jnp.bfloat16))
    return tuple(grads)


def solution(mesh):
    placed = (P(("row", "col", "rep"), None), P(("row", "col", "rep"), None), P(), P(), P(), P())
    return jax.shard_map(
        body,
        mesh=mesh,
        in_specs=placed,
        out_specs=(P(("row", "col", "rep"), None), P(("row", "col", "rep"), None)),
        check_vma=False,
    )
```
